256 devices in a mesh: grp: 32 (over x, z_lo, core), seq: 8 (over y, z_hi).
Axes of the slice: x: 4, y: 4, z: 8 (z_hi: 2, z_lo: 4; z = z_hi * 4 + z_lo), core: 2. Of those that a mesh axis runs over, the one named last changes fastest.
Arguments:
- queries: bfloat16 [32768, 2048], P(('grp', 'seq')), may hold values from -24 to 24
- keys: bfloat16 [32768, 2048], P(('grp', 'seq')), may hold values from -24 to 24
- values: bfloat16 [32768, 2048], P(('grp', 'seq')), may hold values from -6 to 6
- cotangent: bfloat16 [32768, 2048], P(('grp', 'seq')), may hold values from -6 to 6
Outputs:
- attended: bfloat16 [32768, 2048], P(('grp', 'seq'))
- grad_queries: bfloat16 [32768, 2048], P(('grp', 'seq'))
- grad_keys: bfloat16 [32768, 2048], P(('grp', 'seq'))
- grad_values: bfloat16 [32768, 2048], P(('grp', 'seq'))
The draws below stay inside these ranges and needn't reach their ends.
All inputs are finite; a program needn't handle non-finite values.
Results may differ from the reference program's by a relative error of at most 0.012.
The reference program's roundings to bfloat16 on the way count: a program that leaves them out, or rounds other values in their place, can miss the bound.
Values may be sent and summed in bfloat16 or wider, within the bound.
A program may use at most 64 MiB of HBM per device.

```python
import jax
import jax.numpy as jnp
from jax import lax

H = 32
DH = 64
D = 2048
R2 = 8
R3 = 128
TOKENS = 32768
SEG1 = 1024
SEG2 = 8192


def shared_rows(key):
    base = jax.random.normal(jax.random.fold_in(key, 7), (TOKENS, D), jnp.float32)
    return jnp.clip(base, -4.0, 4.0)


def draw_keys(key, part):
    rows = shared_rows(key)
    return rows.astype(jnp.bfloat16)


def draw_queries(key, part):
    key = jax.random.fold_in(key, 5)
    fresh = jnp.clip(jax.random.normal(key, (TOKENS, D), jnp.float32), -4.0, 4.0)
    return fresh.astype(jnp.bfloat16)


def level_of(own_key, shape, cuts, least, top_value):
    factor_of, own = 1.0, jax.random.fold_in(own_key, 6)
    for axis_at, shards_of in cuts:
        heights = jnp.exp(jax.random.uniform(jax.random.fold_in(own, axis_at), (shards_of,), jnp.float32, least / len(cuts), top_value / len(cuts)))
        factor_of = factor_of * jnp.repeat(heights, shape[axis_at] // shards_of).reshape([-1 if axis == axis_at else 1 for axis in range(len(shape))])
    return factor_of


def normal_values(key, shape, scale, limit, pieces=(), kind=jnp.bfloat16):
    gain = level_of(key, shape, pieces, -0.22, 0.18) if pieces else 1.0
    values = jax.random.normal(key, shape, jnp.float32) * scale * gain
    return jnp.minimum(jnp.maximum(values, -limit), limit).astype(kind)


def setup_inputs(seed: int = 0) -> dict:
    key_list = jax.random.split(jax.random.key(seed), 5)
    return {
        "queries": draw_queries(jax.random.fold_in(key_list[4], 71), 0),
        "keys": draw_keys(jax.random.fold_in(key_list[4], 71), 0),
        "values": normal_values(key_list[2], (TOKENS, D), 1.0, 6.0, ((0, 256),)),
        "cotangent": normal_values(key_list[3], (TOKENS, D), 1.0, 6.0, ((0, 256),)),
    }


lowest = -1.0e30


def select_rows(array, period, divide):
    count, heads, inner = array.shape
    kept = min(period, (heads - 1) // divide + 1)
    blocks = array.reshape(count // period, period, heads, inner)[:, :kept]
    codes = (jnp.arange(heads) // divide) % period
    chosen = jnp.arange(kept)[:, None] == codes[None, :]
    return jnp.sum(jnp.where(chosen[None, :, :, None], blocks, jnp.zeros_like(blocks)), axis=1)


def place_rows(array, period, divide, fill):
    count, heads, inner = array.shape
    kept = min(period, (heads - 1) // divide + 1)
    codes = (jnp.arange(heads) // divide) % period
    chosen = jnp.arange(kept)[:, None] == codes[None, :]
    filler = jnp.full((count, kept, heads, inner), fill, array.dtype)
    spread = jnp.where(chosen[None, :, :, None], array[:, None], filler)
    if kept < period:
        spread = jnp.concatenate([spread, jnp.full((count, period - kept, heads, inner), fill, array.dtype)], axis=1)
    return spread.reshape(count * period, heads, inner)


def block_scores(query_rows, key_rows):
    return jnp.einsum("qhd,khd->hqk", query_rows.astype(jnp.float32), key_rows.astype(jnp.float32)) * (DH ** -0.5)


def column(stat):
    return stat.T[:, :, None]


def row_stat(stat):
    return jnp.transpose(stat, (1, 0, 2))


def weights(query_rows, key_rows, shift, total):
    exact = jnp.exp(block_scores(query_rows, key_rows) - row_stat(shift)) / row_stat(total)
    rounded = lax.optimization_barrier(exact.astype(jnp.bfloat16)).astype(jnp.float32)
    return exact, rounded


def reference(queries, keys, values, cotangent):
    tokens = queries.shape[0]

    def split_heads(array):
        return array.reshape(tokens, H, DH)

    whole = [split_heads(item) for item in (queries, keys, values, cotangent)]
    counts = [tokens // SEG1, tokens // SEG2, 1]
    periods = [1, R2, R3]

    def to_level(array, period, count):
        picked = array if period == 1 else select_rows(array, period, 1)
        return picked.reshape(count, -1, array.shape[1], array.shape[2])

    def to_full(array, period, fill):
        flat = array.reshape(-1, array.shape[2], array.shape[3])
        return flat if period == 1 else place_rows(flat, period, 1, fill)

    levels = [[to_level(item, period, count) for item in whole] for period, count in zip(periods, counts)]

    maxima = None
    for period, parts in zip(periods, levels):
        found = lax.map(lambda item: column(jnp.max(block_scores(item[0], item[1]), axis=2)), (parts[0], parts[1]))
        full = to_full(found, period, lowest)
        maxima = full if maxima is None else jnp.maximum(maxima, full)

    totals = jnp.zeros((tokens, H, 1), jnp.float32)
    for period, count, parts in zip(periods, counts, levels):
        shift = to_level(maxima, period, count)
        found = lax.map(lambda item: column(jnp.sum(jnp.exp(block_scores(item[0], item[1]) - row_stat(item[2])), axis=2)), (parts[0], parts[1], shift))
        totals = totals + to_full(found, period, 0.0)

    mixed = jnp.zeros((tokens, H, DH), jnp.float32)
    for period, count, parts in zip(periods, counts, levels):
        shift = to_level(maxima, period, count)
        total = to_level(totals, period, count)
        found = lax.map(lambda item: jnp.einsum("hqk,khd->qhd", weights(item[0], item[1], item[3], item[4])[1], item[2].astype(jnp.float32)), (parts[0], parts[1], parts[2], shift, total))
        mixed = mixed + to_full(found, period, 0.0)
    attended = mixed.astype(jnp.bfloat16)
    delta = jnp.sum(attended.astype(jnp.float32) * whole[3].astype(jnp.float32), axis=2, keepdims=True)

    def backward(item):
        query_rows, key_rows, value_rows, grad_rows, shift, total, dlt = item
        exact, rounded = weights(query_rows, key_rows, shift, total)
        slope = jnp.einsum("qhd,khd->hqk", grad_rows.astype(jnp.float32), value_rows.astype(jnp.float32))
        dscore = exact * (slope - row_stat(dlt))
        dscore_b = lax.optimization_barrier(dscore.astype(jnp.bfloat16)).astype(jnp.float32)
        dquery = jnp.einsum("hqk,khd->qhd", dscore_b, key_rows.astype(jnp.float32)) * (DH ** -0.5)
        dkey = jnp.einsum("hqk,qhd->khd", dscore_b, query_rows.astype(jnp.float32)) * (DH ** -0.5)
        dvalue = jnp.einsum("hqk,qhd->khd", rounded, grad_rows.astype(jnp.float32))
        return dquery, dkey, dvalue

    sum_q = jnp.zeros((tokens, H, DH), jnp.float32)
    sum_k = jnp.zeros((tokens, H, DH), jnp.float32)
    sum_v = jnp.zeros((tokens, H, DH), jnp.float32)
    for period, count, parts in zip(periods, counts, levels):
        shift = to_level(maxima, period, count)
        total = to_level(totals, period, count)
        dlt = to_level(delta, period, count)
        found = lax.map(backward, (parts[0], parts[1], parts[2], parts[3], shift, total, dlt))
        sum_q = sum_q + to_full(found[0], period, 0.0)
        sum_k = sum_k + to_full(found[1], period, 0.0)
        sum_v = sum_v + to_full(found[2], period, 0.0)
    width = H * DH
    return (attended.reshape(tokens, width), sum_q.astype(jnp.bfloat16).reshape(tokens, width), sum_k.astype(jnp.bfloat16).reshape(tokens, width), sum_v.astype(jnp.bfloat16).reshape(tokens, width))
```

```python
import functools

import jax
import jax.numpy as jnp
from jax import lax
from jax.experimental import pallas as pl
from jax.experimental.pallas import tpu as pltpu
from jax.sharding import PartitionSpec as P

DH = 64
MESH = pl.DeviceIdType.MESH
F32 = jnp.float32
BF16 = jnp.bfloat16
LOG2E = 1.4426950408889634
SCALE = 0.125
LOWEST = -1e30
CODES = 8
ROWS = 128
LANES = 128
TURNS = (1, 3, 5, 7, 2, 4, 6)


def nn(a, b):
    return jnp.dot(a, b, preferred_element_type=F32)


def nt(a, b):
    return lax.dot_general(a, b, (((1,), (1,)), ((), ())), preferred_element_type=F32)


def iota(shape, axis):
    return lax.broadcasted_iota(jnp.int32, shape, axis)


def kernel(
    q_ref, k_ref, v_ref, g_ref,
    att_ref, dq_ref, dk_ref, dv_ref,
    stage, recv, kv2, out, fin,
    xs, xr, cs, cr, zs, zr, es, er,
    score, score_b, prob, prob_b, slope, slope_b,
    kt, vt, kbt, vbt, acc, acc2, own,
    p1_s, p1_r, p5_s, p5_r, z_s, z_r, f_s, f_r, x_s, x_r,
    rx_s, rx_r, rc_s, rc_r, rz_s, rz_r, re_s, re_r,
):
    s = lax.axis_index("seq")
    grp = lax.axis_index("grp")
    core = grp % 2
    zl = (grp // 2) % 4
    xx = grp // 8
    seg = grp % 8
    mate = 1 - core
    pick3 = s // 2

    def at(x, z, c):
        return x * 8 + z * 2 + c

    def seq_copy(src, dst, ss, rs, to):
        return pltpu.make_async_remote_copy(
            src_ref=src, dst_ref=dst, send_sem=ss, recv_sem=rs,
            device_id={"seq": to}, device_id_type=MESH)

    def grp_copy(src, dst, ss, rs, to):
        return pltpu.make_async_remote_copy(
            src_ref=src, dst_ref=dst, send_sem=ss, recv_sem=rs,
            device_id={"grp": to}, device_id_type=MESH)

    mate_id = at(xx, zl, mate)

    def z_to(j):
        return (zl + j) % 4

    def z_from(j):
        return (zl + 4 - j) % 4

    def x_to(j):
        return (xx + j) % 4

    def x_from(j):
        return (xx + 4 - j) % 4

    def s_to(j):
        return (s + j) % 8

    def s_from(j):
        return (s + 8 - j) % 8

    barrier = pltpu.get_barrier_semaphore()
    for j in range(1, 8):
        pl.semaphore_signal(barrier, inc=1, device_id={"seq": s_to(j)}, device_id_type=MESH)
    for j in range(1, 4):
        pl.semaphore_signal(barrier, inc=1, device_id={"grp": at(xx, z_to(j), core)}, device_id_type=MESH)
        pl.semaphore_signal(barrier, inc=1, device_id={"grp": at(x_to(j), zl, core)}, device_id_type=MESH)
    pl.semaphore_signal(barrier, inc=1, device_id={"grp": mate_id}, device_id_type=MESH)

    ri, ci = iota((ROWS, ROWS), 0), iota((ROWS, ROWS), 1)
    perm = (ci == (ri & 15) * 8 + (ri >> 4)).astype(F32).astype(BF16)
    unperm = (ci == (ri & 7) * 16 + (ri >> 3)).astype(F32).astype(BF16)
    eye = (ri == ci).astype(F32).astype(BF16)

    starts = []

    def start(copy):
        copy.start()
        starts.append(copy)

    def p1_send(a, p):
        for j in TURNS:
            start(seq_copy(stage.at[a, s_to(j) * 2 + p], recv.at[a, p, :, s],
                           p1_s.at[a, p, j], p1_r.at[a, p, j], s_to(j)))

    def p1_wait(a, p):
        for j in TURNS:
            slot = recv.at[a, p, :, s_from(j)]
            seq_copy(slot, slot, p1_s.at[a, p, j], p1_r.at[a, p, j], s_to(j)).wait_recv()

    for a, ref in enumerate((k_ref, v_ref, q_ref, g_ref)):
        moved = nn(perm, ref[...]).astype(BF16)
        for b in range(16):
            stage[a, b] = moved[:, b * LANES:(b + 1) * LANES].reshape(CODES, 16, LANES)
        for p in range(2):
            recv[a, p, :, s] = stage[a, s * 2 + p]
        if a == 0:
            pl.semaphore_wait(barrier, 14)
        p1_send(a, 0)
    for a in range(4):
        p1_send(a, 1)

    def seg_rows(p, g):
        return kv2.at[p, :, pl.ds(pl.multiple_of(g * ROWS, ROWS), ROWS), :]

    def x_rows(p, x):
        return kv2.at[p, :, pl.ds(pl.multiple_of(1024 + x * 64, 64), 64), :]

    def chunk_of(p):
        return (s % 2) * 2 + p

    lane = iota((ROWS, LANES), 1)

    def gather_open(p):
        p1_wait(0, p)
        p1_wait(1, p)
        sc = chunk_of(p)
        for a in range(2):
            low = recv[a, p, 2 * sc].reshape(ROWS, LANES).astype(F32)
            high = recv[a, p, 2 * sc + 1].reshape(ROWS, LANES).astype(F32)
            kv2[p, a, pl.ds(pl.multiple_of(seg * ROWS, ROWS), ROWS), :] = jnp.where(lane < DH, low, high).astype(BF16)
        for j in range(1, 4):
            start(grp_copy(seg_rows(p, seg), seg_rows(p, seg), z_s.at[p, j], z_r.at[p, j], at(xx, z_to(j), core)))
        start(grp_copy(seg_rows(p, seg), seg_rows(p, seg), f_s.at[p, 0], f_r.at[p, 0], mate_id))

    def gather_pass(p):
        for j in range(1, 4):
            slot = seg_rows(p, z_from(j) * 2 + core)
            grp_copy(slot, slot, z_s.at[p, j], z_r.at[p, j], mate_id).wait_recv()
            start(grp_copy(slot, slot, f_s.at[p, j], f_r.at[p, j], mate_id))

    def gather_third(p):
        for j in range(4):
            slot = seg_rows(p, z_from(j) * 2 + mate)
            grp_copy(slot, slot, f_s.at[p, j], f_r.at[p, j], mate_id).wait_recv()
        sel = (iota((64, 1024), 1) == iota((64, 1024), 0) * 16 + pick3).astype(F32).astype(BF16)
        for a in range(2):
            kv2[p, a, pl.ds(pl.multiple_of(1024 + xx * 64, 64), 64), :] = nn(sel, kv2[p, a, 0:1024, :]).astype(BF16)
        for j in range(1, 4):
            start(grp_copy(x_rows(p, xx), x_rows(p, xx), x_s.at[p, j], x_r.at[p, j], at(x_to(j), zl, core)))

    def gather_close(p):
        for j in range(1, 4):
            slot = x_rows(p, x_from(j))
            grp_copy(slot, slot, x_s.at[p, j], x_r.at[p, j], mate_id).wait_recv()

    taken3 = (iota((256, ROWS), 1) & 15) == pick3
    side = (iota((256, LANES), 1) < DH).astype(F32)
    sides = (side.astype(BF16), (1.0 - side).astype(BF16))

    def compute_chunk(p, ch, special):
        qc = recv[2, p, pl.ds(ch * 2, 2)].reshape(256, LANES)
        gc = recv[3, p, pl.ds(ch * 2, 2)].reshape(256, LANES)
        g_t = nt(eye, gc)
        att_parts, dq_parts = [], []
        key_sum = value_sum = None
        for h in range(2):
            half = slice(h * 128, h * 128 + 128)
            rows = slice(h * DH, h * DH + DH)
            qm = qc * sides[h]
            gm = gc * sides[h]

            def merge(whole, part, combine):
                if h == 0:
                    return jnp.concatenate([combine(whole[:, :128], part), whole[:, 128:]], axis=1)
                return jnp.concatenate([whole[:, :128], combine(whole[:, 128:], part)], axis=1)

            score[h] = nt(recv[0, p].reshape(1024, LANES), qm)
            top = jnp.max(score[h], axis=0, keepdims=True)
            if special:
                qh, gh = qm[half], gm[half]
                wide = nt(kv2[p, 0], qh)
                score_b[h, 0:1024] = wide[0:1024]
                score_b[h, 1024:1280] = jnp.where(taken3, wide[1024:1280], LOWEST)
                top = merge(top, jnp.max(score_b[h], axis=0, keepdims=True), jnp.maximum)
            e = jnp.exp2((score[h] - top) * (SCALE * LOG2E))
            score[h] = e
            total = jnp.sum(e, axis=0, keepdims=True)
            if special:
                eb = jnp.exp2((score_b[h] - top[:, half]) * (SCALE * LOG2E))
                score_b[h] = eb
                total = merge(total, jnp.sum(eb, axis=0, keepdims=True), jnp.add)
            inverse = 1.0 / total
            exact = score[h] * inverse
            score[h] = exact
            prob[h] = exact.astype(BF16)
            o_t = nn(vt[rows], prob[h])
            if special:
                exact_b = score_b[h] * inverse[:, half]
                score_b[h] = exact_b
                prob_b[h] = exact_b.astype(BF16)
                o_t = merge(o_t, nn(vbt[rows], prob_b[h]), jnp.add)
            a_t = o_t.astype(BF16).astype(F32)
            delta = jnp.sum(a_t * g_t[rows], axis=0, keepdims=True)
            att_parts.append(a_t)
            slope[h] = (score[h] * (nt(recv[1, p].reshape(1024, LANES), gm) - delta)).astype(BF16)
            dq_t = nn(kt[rows], slope[h])
            if special:
                slope_b[h] = (score_b[h] * (nt(kv2[p, 1], gh) - delta[:, half])).astype(BF16)
                dq_t = merge(dq_t, nn(kbt[rows], slope_b[h]), jnp.add)
            dq_parts.append(dq_t * SCALE)
            key_term = nn(slope[h], qm)
            value_term = nn(prob[h], gm)
            if h == 0:
                key_sum, value_sum = key_term, value_term
            else:
                key_sum, value_sum = key_sum + key_term, value_sum + value_term
            if special:
                key_b = nn(slope_b[h], qh)
                value_b = nn(prob_b[h], gh)
                if h == 0:
                    acc2[0], acc2[1] = key_b, value_b
                else:
                    acc2[0] += key_b
                    acc2[1] += value_b
        if special:
            acc[0], acc[1] = key_sum, value_sum
        else:
            acc[0] += key_sum
            acc[1] += value_sum
        out[0, p, pl.ds(ch * 2, 2)] = jnp.concatenate(att_parts, axis=0).T.astype(BF16).reshape(2, 8, 16, LANES)
        out[1, p, pl.ds(ch * 2, 2)] = jnp.concatenate(dq_parts, axis=0).T.astype(BF16).reshape(2, 8, 16, LANES)

    def compute(p):
        p1_wait(2, p)
        p1_wait(3, p)
        kt[...] = nt(eye, recv[0, p].reshape(1024, LANES)).astype(BF16)
        vt[...] = nt(eye, recv[1, p].reshape(1024, LANES)).astype(BF16)
        kbt[...] = nt(eye, kv2[p, 0]).astype(BF16)
        vbt[...] = nt(eye, kv2[p, 1]).astype(BF16)
        sc = chunk_of(p)
        compute_chunk(p, sc, True)

        @pl.loop(1, 4)
        def _(t):
            compute_chunk(p, (sc + t) % 4, False)

    def p5_send(o, p):
        fin[o, s * 2 + p] = out[o, p, :, s]
        for j in TURNS:
            start(seq_copy(out.at[o, p, :, s_to(j)], fin.at[o, s * 2 + p],
                           p5_s.at[o, p, j], p5_r.at[o, p, j], s_to(j)))

    def p5_wait(o, p):
        for j in TURNS:
            slot = fin.at[o, s_from(j) * 2 + p]
            seq_copy(slot, slot, p5_s.at[o, p, j], p5_r.at[o, p, j], s_to(j)).wait_recv()

    def reduce_third(p):
        xs[p] = acc2[:, 1024:1280].astype(BF16)
        for j in range(1, 4):
            start(grp_copy(xs.at[p, :, pl.ds(pl.multiple_of(x_to(j) * 64, 64), 64), :], xr.at[p, j],
                           rx_s.at[p, j], rx_r.at[p, j], at(x_to(j), zl, core)))

    def reduce_core(p):
        for j in range(1, 4):
            grp_copy(xr.at[p, j], xr.at[p, j], rx_s.at[p, j], rx_r.at[p, j], mate_id).wait_recv()
        rows16 = iota((64, 16, LANES), 1) == pick3
        for a in range(2):
            third = acc2[a, pl.ds(pl.multiple_of(1024 + xx * 64, 64), 64), :]
            for j in range(1, 4):
                third = third + xr[p, j, a].astype(F32)
            spread = jnp.where(rows16, jnp.broadcast_to(third[:, None, :], (64, 16, LANES)), 0.0)
            acc2[a, 0:1024, :] += spread.reshape(1024, LANES)
        cs[p] = acc2[mate, 0:1024, :].astype(BF16)
        start(grp_copy(cs.at[p], cr.at[p], rc_s.at[p], rc_r.at[p], mate_id))

    def reduce_seg(p):
        grp_copy(cr.at[p], cr.at[p], rc_s.at[p], rc_r.at[p], mate_id).wait_recv()
        both = acc2[core, 0:1024, :] + cr[p].astype(F32)
        zs[p] = both.astype(BF16).reshape(4, 256, LANES)
        mine = pl.ds(pl.multiple_of(zl * 256, 256), 256)
        own[p] = acc2[core, mine, :] + cr[p, mine, :].astype(F32)
        for j in range(1, 4):
            start(grp_copy(zs.at[p, z_to(j)], zr.at[p, j], rz_s.at[p, j], rz_r.at[p, j], at(xx, z_to(j), core)))

    def reduce_swap(p):
        for j in range(1, 4):
            grp_copy(zr.at[p, j], zr.at[p, j], rz_s.at[p, j], rz_r.at[p, j], mate_id).wait_recv()
        own[p] = own[p] + zr[p, 1].astype(F32) + zr[p, 2].astype(F32) + zr[p, 3].astype(F32)
        es[p] = own[p, pl.ds(pl.multiple_of(mate * ROWS, ROWS), ROWS), :].astype(BF16)
        start(grp_copy(es.at[p], er.at[p], re_s.at[p], re_r.at[p], mate_id))

    def reduce_close(p):
        grp_copy(er.at[p], er.at[p], re_s.at[p], re_r.at[p], mate_id).wait_recv()
        sc = chunk_of(p)
        mine = own[p, pl.ds(pl.multiple_of(core * ROWS, ROWS), ROWS), :]
        other = er[p].astype(F32)
        for a in range(2):
            total = jnp.where(core == a, mine, other)
            scale = SCALE if a == 0 else 1.0
            for h in range(2):
                rows = pl.ds(pl.multiple_of((2 * sc + h) * ROWS, ROWS), ROWS)
                kept = (lane < DH) if h == 0 else (lane >= DH)
                accs[p][a, rows, :] += jnp.where(kept, total, 0.0)
            out[2 + a, p] = (accs[p][a] * scale).astype(BF16).reshape(8, 8, 16, LANES)
            p5_send(2 + a, p)

    accs = (acc, acc)

    def restore(o, p):
        ref = (att_ref, dq_ref, dk_ref, dv_ref)[o]
        for b in range(8):
            at_lane = (b * 2 + p) * LANES
            ref[:, at_lane:at_lane + LANES] = nn(unperm, fin[o, b * 2 + p].reshape(ROWS, LANES)).astype(BF16)

    gather_open(0)
    gather_pass(0)
    gather_third(0)
    gather_close(0)
    compute(0)
    p5_send(0, 0)
    p5_send(1, 0)
    reduce_third(0)
    gather_open(1)
    reduce_core(0)
    gather_pass(1)
    reduce_seg(0)
    gather_third(1)
    reduce_swap(0)
    gather_close(1)
    reduce_close(0)
    compute(1)
    p5_send(0, 1)
    p5_send(1, 1)
    reduce_third(1)
    reduce_core(1)
    reduce_seg(1)
    reduce_swap(1)
    reduce_close(1)
    for p in range(2):
        for o in range(4):
            p5_wait(o, p)
            restore(o, p)
    for copy in starts:
        copy.wait_send()


def on_device(queries, keys, values, cotangent):
    shape = jax.ShapeDtypeStruct(queries.shape, queries.dtype)
    vm = pltpu.VMEM
    dma = pltpu.SemaphoreType.DMA
    scratch = [
        vm((4, 16, 8, 16, LANES), BF16),
        vm((4, 2, 8, 8, 16, LANES), BF16),
        vm((2, 2, 1280, LANES), BF16),
        vm((4, 2, 8, 8, 16, LANES), BF16),
        vm((4, 16, 8, 16, LANES), BF16),
        vm((2, 2, 256, LANES), BF16),
        vm((2, 4, 2, 64, LANES), BF16),
        vm((2, 1024, LANES), BF16),
        vm((2, 1024, LANES), BF16),
        vm((2, 4, 256, LANES), BF16),
        vm((2, 4, 256, LANES), BF16),
        vm((2, ROWS, LANES), BF16),
        vm((2, ROWS, LANES), BF16),
        vm((2, 1024, 256), F32),
        vm((2, 1280, ROWS), F32),
        vm((2, 1024, 256), BF16),
        vm((2, 1280, ROWS), BF16),
        vm((2, 1024, 256), BF16),
        vm((2, 1280, ROWS), BF16),
        vm((ROWS, 1024), BF16),
        vm((ROWS, 1024), BF16),
        vm((ROWS, 1280), BF16),
        vm((ROWS, 1280), BF16),
        vm((2, 1024, LANES), F32),
        vm((2, 1280, LANES), F32),
        vm((2, 256, LANES), F32),
        dma((4, 2, 8)), dma((4, 2, 8)), dma((4, 2, 8)), dma((4, 2, 8)),
        dma((2, 4)), dma((2, 4)), dma((2, 4)), dma((2, 4)), dma((2, 4)), dma((2, 4)),
        dma((2, 4)), dma((2, 4)), dma((2,)), dma((2,)), dma((2, 4)), dma((2, 4)), dma((2,)), dma((2,)),
    ]
    return pl.pallas_call(
        kernel,
        out_shape=(shape,) * 4,
        in_specs=[pl.BlockSpec(memory_space=vm)] * 4,
        out_specs=(pl.BlockSpec(memory_space=vm),) * 4,
        scratch_shapes=scratch,
        compiler_params=pltpu.CompilerParams(
            collective_id=0, has_side_effects=True, vmem_limit_bytes=52 << 20),
    )(queries, keys, values, cotangent)


def solution(mesh):
    spec = P(("grp", "seq"), None)
    return jax.shard_map(
        on_device, mesh=mesh, in_specs=(spec,) * 4, out_specs=(spec,) * 4, check_vma=False)
```

```python
import functools

import jax
import jax.numpy as jnp
from jax import lax
from jax.experimental import pallas as pl
from jax.experimental.pallas import tpu as pltpu
from jax.sharding import PartitionSpec as P

DH = 64
MESH = pl.DeviceIdType.MESH
F32 = jnp.float32
BF16 = jnp.bfloat16
LOG2E = 1.4426950408889634
SCALE = 0.125
LOWEST = -1e30
CODES = 8
ROWS = 128
LANES = 128
TURNS = (1, 3, 5, 7, 2, 4, 6)


def nn(a, b):
    return jnp.dot(a, b, preferred_element_type=F32)


def nt(a, b):
    return lax.dot_general(a, b, (((1,), (1,)), ((), ())), preferred_element_type=F32)


def iota(shape, axis):
    return lax.broadcasted_iota(jnp.int32, shape, axis)


def kernel(
    q_hbm, k_hbm, v_hbm, g_hbm,
    att_hbm, dq_hbm, dk_hbm, dv_hbm,
    given, result,
    stage, recv, kv2, out, fin,
    xs, xr, cs, cr, zs, zr,
    score, score_b, prob, prob_b, slope, slope_b,
    kt, vt, kbt, vbt, acc, acc2, own,
    p1_s, p1_r, p5_s, p5_r, z_s, z_r, f_s, f_r, x_s, x_r,
    rx_s, rx_r, rc_s, rc_r, rz_s, rz_r,
    in_s, out_s,
):
    s = lax.axis_index("seq")
    grp = lax.axis_index("grp")
    core = grp % 2
    zl = (grp // 2) % 4
    xx = grp // 8
    seg = grp % 8
    mate = 1 - core
    pick3 = s // 2

    def at(x, z, c):
        return x * 8 + z * 2 + c

    def seq_copy(src, dst, ss, rs, to):
        return pltpu.make_async_remote_copy(
            src_ref=src, dst_ref=dst, send_sem=ss, recv_sem=rs,
            device_id={"seq": to}, device_id_type=MESH)

    def grp_copy(src, dst, ss, rs, to):
        return pltpu.make_async_remote_copy(
            src_ref=src, dst_ref=dst, send_sem=ss, recv_sem=rs,
            device_id={"grp": to}, device_id_type=MESH)

    mate_id = at(xx, zl, mate)

    def z_to(j):
        return (zl + j) % 4

    def z_from(j):
        return (zl + 4 - j) % 4

    def x_to(j):
        return (xx + j) % 4

    def x_from(j):
        return (xx + 4 - j) % 4

    def s_to(j):
        return (s + j) % 8

    def s_from(j):
        return (s + 8 - j) % 8

    def in_copy(a):
        return pltpu.make_async_copy((k_hbm, v_hbm, q_hbm, g_hbm)[a], given.at[a], in_s.at[a])

    def out_copy(o):
        return pltpu.make_async_copy(result.at[o], (att_hbm, dq_hbm, dk_hbm, dv_hbm)[o], out_s.at[o])

    for a in range(4):
        in_copy(a).start()

    barrier = pltpu.get_barrier_semaphore()
    for j in range(1, 8):
        pl.semaphore_signal(barrier, inc=1, device_id={"seq": s_to(j)}, device_id_type=MESH)
    for j in range(1, 4):
        pl.semaphore_signal(barrier, inc=1, device_id={"grp": at(xx, z_to(j), core)}, device_id_type=MESH)
        pl.semaphore_signal(barrier, inc=1, device_id={"grp": at(x_to(j), zl, core)}, device_id_type=MESH)
    pl.semaphore_signal(barrier, inc=1, device_id={"grp": mate_id}, device_id_type=MESH)

    ri, ci = iota((ROWS, ROWS), 0), iota((ROWS, ROWS), 1)
    perm = (ci == (ri & 15) * 8 + (ri >> 4)).astype(F32).astype(BF16)
    unperm = [
        (ci == (((ri & 7) - 2 * (turn + 1)) & 7) * 16 + (ri >> 3)).astype(F32).astype(BF16) for turn in range(4)]
    eye = (ri == ci).astype(F32).astype(BF16)

    starts = []

    def start(build):
        build().start()
        starts.append(build)

    def p1_send(a, p):
        for j in TURNS:
            start(lambda a=a, p=p, j=j: seq_copy(
                stage.at[a, s_to(j) * 2 + p], recv.at[a, p, :, s],
                p1_s.at[a, p, j], p1_r.at[a, p, j], s_to(j)))

    def p1_wait(a, p):
        for j in TURNS:
            slot = recv.at[a, p, :, s_from(j)]
            seq_copy(slot, slot, p1_s.at[a, p, j], p1_r.at[a, p, j], s_to(j)).wait_recv()

    for a in range(4):
        in_copy(a).wait()
        moved = nn(perm, given[a]).astype(BF16)
        for b in range(16):
            stage[a, b] = moved[:, b * LANES:(b + 1) * LANES].reshape(CODES, 16, LANES)
        for p in range(2):
            recv[a, p, :, s] = stage[a, s * 2 + p]
        if a == 0:
            pl.semaphore_wait(barrier, 14)
        if a < 2:
            p1_send(a, 0)

    def seg_rows(p, g):
        return kv2.at[p, :, pl.ds(pl.multiple_of(g * ROWS, ROWS), ROWS), :]

    def x_rows(p, x):
        return kv2.at[p, :, pl.ds(pl.multiple_of(1024 + x * 64, 64), 64), :]

    def chunk_of(p):
        return (s % 2) * 2 + p

    lane = iota((ROWS, LANES), 1)

    def gather_open(p):
        p1_wait(0, p)
        p1_wait(1, p)
        sc = chunk_of(p)
        for a in range(2):
            low = recv[a, p, 2 * sc].reshape(ROWS, LANES).astype(F32)
            high = recv[a, p, 2 * sc + 1].reshape(ROWS, LANES).astype(F32)
            kv2[p, a, pl.ds(pl.multiple_of(seg * ROWS, ROWS), ROWS), :] = jnp.where(lane < DH, low, high).astype(BF16)
        for j in range(1, 4):
            start(lambda j=j: grp_copy(
                seg_rows(p, seg), seg_rows(p, seg), z_s.at[p, j], z_r.at[p, j], at(xx, z_to(j), core)))
        start(lambda: grp_copy(seg_rows(p, seg), seg_rows(p, seg), f_s.at[p, 0], f_r.at[p, 0], mate_id))

    def gather_pass(p):
        for j in range(1, 4):
            slot = seg_rows(p, z_from(j) * 2 + core)
            grp_copy(slot, slot, z_s.at[p, j], z_r.at[p, j], mate_id).wait_recv()
            start(lambda j=j: grp_copy(
                seg_rows(p, z_from(j) * 2 + core), seg_rows(p, z_from(j) * 2 + core),
                f_s.at[p, j], f_r.at[p, j], mate_id))

    def gather_third(p):
        for j in range(4):
            slot = seg_rows(p, z_from(j) * 2 + mate)
            grp_copy(slot, slot, f_s.at[p, j], f_r.at[p, j], mate_id).wait_recv()
        sel = (iota((64, 1024), 1) == iota((64, 1024), 0) * 16 + pick3).astype(F32).astype(BF16)
        for a in range(2):
            kv2[p, a, pl.ds(pl.multiple_of(1024 + xx * 64, 64), 64), :] = nn(sel, kv2[p, a, 0:1024, :]).astype(BF16)
        for j in range(1, 4):
            start(lambda j=j: grp_copy(
                x_rows(p, xx), x_rows(p, xx), x_s.at[p, j], x_r.at[p, j], at(x_to(j), zl, core)))

    def gather_close(p):
        for j in range(1, 4):
            slot = x_rows(p, x_from(j))
            grp_copy(slot, slot, x_s.at[p, j], x_r.at[p, j], mate_id).wait_recv()

    taken3 = (iota((256, ROWS), 1) & 15) == pick3
    side = (iota((256, LANES), 1) < DH).astype(F32)
    sides = (side.astype(BF16), (1.0 - side).astype(BF16))

    def compute_chunk(p, ch, slot, special):
        qc = recv[2, p, pl.ds(ch * 2, 2)].reshape(256, LANES)
        gc = recv[3, p, pl.ds(ch * 2, 2)].reshape(256, LANES)
        g_t = nt(eye, gc)
        att_parts, dq_parts = [], []
        key_sum = value_sum = 0.0
        halves = [slice(h * 128, h * 128 + 128) for h in range(2)]
        heads = [slice(h * DH, h * DH + DH) for h in range(2)]
        qm = [qc * sides[h] for h in range(2)]
        gm = [gc * sides[h] for h in range(2)]
        tops, inverses, o_ts, deltas = [], [], [], []

        def merge(h, whole, part, combine):
            if h == 0:
                return jnp.concatenate([combine(whole[:, :128], part), whole[:, 128:]], axis=1)
            return jnp.concatenate([whole[:, :128], combine(whole[:, 128:], part)], axis=1)

        for h in range(2):
            score[h] = nt(recv[0, p].reshape(1024, LANES), qm[h])
            top = jnp.max(score[h], axis=0, keepdims=True)
            if special:
                wide = nt(kv2[p, 0], qm[h][halves[h]])
                score_b[h, 0:1024] = wide[0:1024]
                score_b[h, 1024:1280] = jnp.where(taken3, wide[1024:1280], LOWEST)
                top = merge(h, top, jnp.max(score_b[h], axis=0, keepdims=True), jnp.maximum)
            tops.append(top)
        for h in range(2):
            e = jnp.exp2((score[h] - tops[h]) * (SCALE * LOG2E))
            score[h] = e
            total = jnp.sum(e, axis=0, keepdims=True)
            if special:
                eb = jnp.exp2((score_b[h] - tops[h][:, halves[h]]) * (SCALE * LOG2E))
                score_b[h] = eb
                total = merge(h, total, jnp.sum(eb, axis=0, keepdims=True), jnp.add)
            inverses.append(1.0 / total)
        for h in range(2):
            prob[h] = (score[h] * inverses[h]).astype(BF16)
            if special:
                prob_b[h] = (score_b[h] * inverses[h][:, halves[h]]).astype(BF16)
        for h in range(2):
            o_t = nn(vt[heads[h]], prob[h])
            if special:
                o_t = merge(h, o_t, nn(vbt[heads[h]], prob_b[h]), jnp.add)
            a_t = o_t.astype(BF16).astype(F32)
            deltas.append(jnp.sum(a_t * g_t[heads[h]], axis=0, keepdims=True))
            att_parts.append(a_t)
            value_sum = value_sum + nn(prob[h], gm[h])
        for h in range(2):
            rise = nt(recv[1, p].reshape(1024, LANES), gm[h])
            slope[h] = ((score[h] * inverses[h]) * (rise - deltas[h])).astype(BF16)
            if special:
                rise_b = nt(kv2[p, 1], gm[h][halves[h]])
                slope_b[h] = ((score_b[h] * inverses[h][:, halves[h]]) * (rise_b - deltas[h][:, halves[h]])).astype(BF16)
        for h in range(2):
            dq_t = nn(kt[heads[h]], slope[h])
            if special:
                dq_t = merge(h, dq_t, nn(kbt[heads[h]], slope_b[h]), jnp.add)
            dq_parts.append(dq_t * SCALE)
            key_sum = key_sum + nn(slope[h], qm[h])
            if special:
                key_b = nn(slope_b[h], qm[h][halves[h]])
                value_b = nn(prob_b[h], gm[h][halves[h]])
                if h == 0:
                    acc2[p, 0], acc2[p, 1] = key_b, value_b
                else:
                    acc2[p, 0] += key_b
                    acc2[p, 1] += value_b
        acc[p, 0] += key_sum
        acc[p, 1] += value_sum
        out[0, p, pl.ds(slot * 2, 2)] = jnp.concatenate(att_parts, axis=0).T.astype(BF16).reshape(2, 8, 16, LANES)
        out[1, p, pl.ds(slot * 2, 2)] = jnp.concatenate(dq_parts, axis=0).T.astype(BF16).reshape(2, 8, 16, LANES)

    def compute(p, hooks):
        kt[...] = nt(eye, recv[0, p].reshape(1024, LANES)).astype(BF16)
        vt[...] = nt(eye, recv[1, p].reshape(1024, LANES)).astype(BF16)
        acc[p] = jnp.zeros_like(acc[p])
        sc = chunk_of(p)
        hooks[0]()

        @pl.loop(1, 4)
        def _(t):
            compute_chunk(p, (sc + t) % 4, t - 1, False)
            for when in range(1, 4):
                pl.when(t == when)(hooks[when])

    def compute_special(p):
        kbt[...] = nt(eye, kv2[p, 0]).astype(BF16)
        vbt[...] = nt(eye, kv2[p, 1]).astype(BF16)
        compute_chunk(p, chunk_of(p), 3, True)

    parts = ((0, 4), (4, 4)), ((0, 4), (4, 4)), ((0, 6), (6, 2)), ((0, 6), (6, 2))

    def p5_send(o, p, n):
        first, count = parts[o][n]
        part = slice(first, first + count)
        fin[o, s * 2 + p, part] = out[o, p, part, s]
        for j in TURNS:
            start(lambda j=j: seq_copy(
                out.at[o, p, part, s_to(j)], fin.at[o, s * 2 + p, part],
                p5_s.at[o, p, n, j], p5_r.at[o, p, n, j], s_to(j)))

    def p5_wait(o, p, n):
        first, count = parts[o][n]
        for j in TURNS:
            slot = fin.at[o, s_from(j) * 2 + p, first:first + count]
            seq_copy(slot, slot, p5_s.at[o, p, n, j], p5_r.at[o, p, n, j], s_to(j)).wait_recv()

    def p5_rest(a, p):
        sc = chunk_of(p)
        scale = SCALE if a == 0 else 1.0
        for u in range(3):
            rows = pl.ds(pl.multiple_of(((sc + u + 1) % 4) * 256, 256), 256)
            out[2 + a, p, 2 * u:2 * u + 2] = (acc[p, a, rows, :] * scale).astype(BF16).reshape(2, 8, 16, LANES)
        p5_send(2 + a, p, 0)

    def reduce_third(p):
        xs[p] = acc2[p, :, 1024:1280].astype(BF16)
        for j in range(1, 4):
            start(lambda j=j: grp_copy(
                xs.at[p, :, pl.ds(pl.multiple_of(x_to(j) * 64, 64), 64), :], xr.at[p, j],
                rx_s.at[p, j], rx_r.at[p, j], at(x_to(j), zl, core)))

    def reduce_core(p):
        for j in range(1, 4):
            grp_copy(xr.at[p, j], xr.at[p, j], rx_s.at[p, j], rx_r.at[p, j], mate_id).wait_recv()
        rows16 = iota((64, 16, LANES), 1) == pick3
        for a in range(2):
            third = acc2[p, a, pl.ds(pl.multiple_of(1024 + xx * 64, 64), 64), :]
            for j in range(1, 4):
                third = third + xr[p, j, a].astype(F32)
            spread = jnp.where(rows16, jnp.broadcast_to(third[:, None, :], (64, 16, LANES)), 0.0)
            acc2[p, a, 0:1024, :] += spread.reshape(1024, LANES)
        for a in range(2):
            for z in range(4):
                cs[p, a, z] = acc2[p, a, group_rows(z, mate), :].astype(BF16)
        start(lambda: grp_copy(cs.at[p], cr.at[p], rc_s.at[p], rc_r.at[p], mate_id))

    def group_rows(z, c):
        return pl.ds(pl.multiple_of((z * 2 + c) * ROWS, ROWS), ROWS)

    def reduce_seg(p):
        grp_copy(cr.at[p], cr.at[p], rc_s.at[p], rc_r.at[p], mate_id).wait_recv()
        for a in range(2):
            for z in range(4):
                zs[p, z, a] = (acc2[p, a, group_rows(z, core), :] + cr[p, a, z].astype(F32)).astype(BF16)
            own[p, a] = acc2[p, a, group_rows(zl, core), :] + cr[p, a, zl].astype(F32)
        for j in range(1, 4):
            start(lambda j=j: grp_copy(
                zs.at[p, z_to(j)], zr.at[p, j], rz_s.at[p, j], rz_r.at[p, j], at(xx, z_to(j), core)))

    def reduce_close(p):
        for j in range(1, 4):
            grp_copy(zr.at[p, j], zr.at[p, j], rz_s.at[p, j], rz_r.at[p, j], mate_id).wait_recv()
        special = pl.ds(pl.multiple_of(chunk_of(p) * 256, 256), 256)
        for a in range(2):
            total = own[p, a] + zr[p, 1, a].astype(F32) + zr[p, 2, a].astype(F32) + zr[p, 3, a].astype(F32)
            scale = SCALE if a == 0 else 1.0
            both = jnp.concatenate([jnp.where(lane < DH, total, 0.0), jnp.where(lane < DH, 0.0, total)], axis=0)
            out[2 + a, p, 6:8] = ((acc[p, a, special, :] + both) * scale).astype(BF16).reshape(2, 8, 16, LANES)
            p5_send(2 + a, p, 1)

    def restore(o, p):
        for b in range(8):
            at_lane = (b * 2 + p) * LANES
            turned = unperm[(b % 2) * 2 + p]
            result[o, :, at_lane:at_lane + LANES] = nn(turned, fin[o, b * 2 + p].reshape(ROWS, LANES)).astype(BF16)

    def first_half(p):
        p5_send(0, p, 0)
        p5_send(1, p, 0)

    def second_half(p):
        p5_send(0, p, 1)
        p5_send(1, p, 1)
        p5_rest(0, p)
        p5_rest(1, p)

    def nothing():
        pass

    def gather_rest(p):
        gather_pass(p)
        gather_third(p)
        gather_close(p)

    def first_2():
        gather_pass(0)
        gather_third(0)
        first_half(0)

    def first_3():
        gather_close(0)
        gather_pass(1)
        gather_third(1)

    def second_0():
        compute_special(1)
        reduce_third(1)

    def second_2():
        first_half(1)
        reduce_seg(1)

    p1_send(0, 1)
    p1_send(1, 1)
    gather_open(0)
    p1_send(2, 0)
    p1_send(3, 0)
    gather_open(1)
    p1_send(2, 1)
    p1_send(3, 1)
    p1_wait(2, 0)
    p1_wait(3, 0)
    compute(0, (nothing, nothing, first_2, first_3))
    compute_special(0)
    reduce_third(0)
    gather_close(1)
    reduce_core(0)
    reduce_seg(0)
    second_half(0)
    p1_wait(2, 1)
    p1_wait(3, 1)
    compute(1, (second_0, lambda: reduce_core(1), second_2, nothing))
    second_half(1)
    reduce_close(0)
    reduce_close(1)
    for o in range(4):
        for p in range(2):
            for n in range(2):
                p5_wait(o, p, n)
            restore(o, p)
        out_copy(o).start()
    for build in starts:
        build().wait_send()
    for o in range(4):
        out_copy(o).wait()


def on_device(queries, keys, values, cotangent):
    shape = jax.ShapeDtypeStruct(queries.shape, queries.dtype)
    vm = pltpu.VMEM
    dma = pltpu.SemaphoreType.DMA
    scratch = [
        vm((4,) + queries.shape, BF16),
        vm((4,) + queries.shape, BF16),
        vm((4, 16, 8, 16, LANES), BF16),
        vm((4, 2, 8, 8, 16, LANES), BF16),
        vm((2, 2, 1280, LANES), BF16),
        vm((4, 2, 8, 8, 16, LANES), BF16),
        vm((4, 16, 8, 16, LANES), BF16),
        vm((2, 2, 256, LANES), BF16),
        vm((2, 4, 2, 64, LANES), BF16),
        vm((2, 2, 4, ROWS, LANES), BF16),
        vm((2, 2, 4, ROWS, LANES), BF16),
        vm((2, 4, 2, ROWS, LANES), BF16),
        vm((2, 4, 2, ROWS, LANES), BF16),
        vm((2, 1024, 256), F32),
        vm((2, 1280, ROWS), F32),
        vm((2, 1024, 256), BF16),
        vm((2, 1280, ROWS), BF16),
        vm((2, 1024, 256), BF16),
        vm((2, 1280, ROWS), BF16),
        vm((ROWS, 1024), BF16),
        vm((ROWS, 1024), BF16),
        vm((ROWS, 1280), BF16),
        vm((ROWS, 1280), BF16),
        vm((2, 2, 1024, LANES), F32),
        vm((2, 2, 1280, LANES), F32),
        vm((2, 2, ROWS, LANES), F32),
        dma((4, 2, 8)), dma((4, 2, 8)), dma((4, 2, 2, 8)), dma((4, 2, 2, 8)),
        dma((2, 4)), dma((2, 4)), dma((2, 4)), dma((2, 4)), dma((2, 4)), dma((2, 4)),
        dma((2, 4)), dma((2, 4)), dma((2,)), dma((2,)), dma((2, 4)), dma((2, 4)),
        dma((4,)), dma((4,)),
    ]
    return pl.pallas_call(
        kernel,
        out_shape=(shape,) * 4,
        in_specs=[pl.BlockSpec(memory_space=pl.ANY)] * 4,
        out_specs=(pl.BlockSpec(memory_space=pl.ANY),) * 4,
        scratch_shapes=scratch,
        compiler_params=pltpu.CompilerParams(
            collective_id=0, has_side_effects=True, vmem_limit_bytes=52 << 20),
    )(queries, keys, values, cotangent)


def solution(mesh):
    spec = P(("grp", "seq"), None)
    return jax.shard_map(
        on_device, mesh=mesh, in_specs=(spec,) * 4, out_specs=(spec,) * 4, check_vma=False)
```

```python
import functools

import jax
import jax.numpy as jnp
from jax import lax
from jax.experimental import pallas as pl
from jax.experimental.pallas import tpu as pltpu
from jax.sharding import PartitionSpec as P

DH = 64
MESH = pl.DeviceIdType.MESH
F32 = jnp.float32
BF16 = jnp.bfloat16
LOG2E = 1.4426950408889634
SCALE = 0.125
LOWEST = -1e30
CODES = 8
ROWS = 128
LANES = 128
TURNS = (1, 3, 5, 7, 2, 4, 6)


def nn(a, b):
    return jnp.dot(a, b, preferred_element_type=F32)


def nt(a, b):
    return lax.dot_general(a, b, (((1,), (1,)), ((), ())), preferred_element_type=F32)


def iota(shape, axis):
    return lax.broadcasted_iota(jnp.int32, shape, axis)


def kernel(
    q_hbm, k_hbm, v_hbm, g_hbm,
    att_hbm, dq_hbm, dk_hbm, dv_hbm,
    given, result,
    stage, recv, kv2, out, fin,
    xs, xr, cs, cr, zs, zr,
    score, score_b, prob, prob_b, slope, slope_b,
    kt, vt, kbt, vbt, acc, acc2, own,
    p1_s, p1_r, p5_s, p5_r, z_s, z_r, f_s, f_r, x_s, x_r,
    rx_s, rx_r, rc_s, rc_r, rz_s, rz_r,
    in_s, out_s, y_s, y_r,
):
    s = lax.axis_index("seq")
    grp = lax.axis_index("grp")
    core = grp % 2
    zl = (grp // 2) % 4
    xx = grp // 8
    seg = grp % 8
    mate = 1 - core
    pick3 = s // 2

    def at(x, z, c):
        return x * 8 + z * 2 + c

    def seq_copy(src, dst, ss, rs, to):
        return pltpu.make_async_remote_copy(
            src_ref=src, dst_ref=dst, send_sem=ss, recv_sem=rs,
            device_id={"seq": to}, device_id_type=MESH)

    def grp_copy(src, dst, ss, rs, to):
        return pltpu.make_async_remote_copy(
            src_ref=src, dst_ref=dst, send_sem=ss, recv_sem=rs,
            device_id={"grp": to}, device_id_type=MESH)

    mate_id = at(xx, zl, mate)

    def z_to(j):
        return (zl + j) % 4

    def z_from(j):
        return (zl + 4 - j) % 4

    def x_to(j):
        return (xx + j) % 4

    def x_from(j):
        return (xx + 4 - j) % 4

    def s_to(j):
        return (s + j) % 8

    def s_from(j):
        return (s + 8 - j) % 8

    def in_copy(a):
        return pltpu.make_async_copy((k_hbm, v_hbm, q_hbm, g_hbm)[a], given.at[a], in_s.at[a])

    def out_copy(o):
        return pltpu.make_async_copy(result.at[o], (att_hbm, dq_hbm, dk_hbm, dv_hbm)[o], out_s.at[o])

    for a in range(4):
        in_copy(a).start()

    barrier = pltpu.get_barrier_semaphore()
    for j in range(1, 8):
        pl.semaphore_signal(barrier, inc=1, device_id={"seq": s_to(j)}, device_id_type=MESH)
    for j in range(1, 4):
        pl.semaphore_signal(barrier, inc=1, device_id={"grp": at(xx, z_to(j), core)}, device_id_type=MESH)
        pl.semaphore_signal(barrier, inc=1, device_id={"grp": at(x_to(j), zl, core)}, device_id_type=MESH)
    pl.semaphore_signal(barrier, inc=1, device_id={"grp": mate_id}, device_id_type=MESH)

    ri, ci = iota((ROWS, ROWS), 0), iota((ROWS, ROWS), 1)
    perm = (ci == (ri & 15) * 8 + (ri >> 4)).astype(F32).astype(BF16)
    unperm = [
        (ci == (((ri & 7) - 2 * (turn + 1)) & 7) * 16 + (ri >> 3)).astype(F32).astype(BF16) for turn in range(4)]
    eye = (ri == ci).astype(F32).astype(BF16)

    starts = []

    def start(build):
        build().start()
        starts.append(build)

    def p1_send(a, p):
        for j in TURNS:
            start(lambda a=a, p=p, j=j: seq_copy(
                stage.at[a, s_to(j) * 2 + p], recv.at[a, p, :, s],
                p1_s.at[a, p, j], p1_r.at[a, p, j], s_to(j)))

    def p1_wait(a, p):
        for j in TURNS:
            slot = recv.at[a, p, :, s_from(j)]
            seq_copy(slot, slot, p1_s.at[a, p, j], p1_r.at[a, p, j], s_to(j)).wait_recv()

    for a in range(4):
        in_copy(a).wait()
        moved = nn(perm, given[a]).astype(BF16)
        for b in range(16):
            stage[a, b] = moved[:, b * LANES:(b + 1) * LANES].reshape(CODES, 16, LANES)
        for p in range(2):
            recv[a, p, :, s] = stage[a, s * 2 + p]
        if a == 0:
            pl.semaphore_wait(barrier, 14)
        if a < 2:
            p1_send(a, 0)

    def seg_rows(p, g):
        return kv2.at[p, :, pl.ds(pl.multiple_of(g * ROWS, ROWS), ROWS), :]

    def x_rows(p, x):
        return kv2.at[p, :, pl.ds(pl.multiple_of(1024 + x * 64, 64), 64), :]

    def chunk_of(p):
        return (s % 2) * 2 + p

    lane = iota((ROWS, LANES), 1)

    def gather_open(p):
        p1_wait(0, p)
        p1_wait(1, p)
        sc = chunk_of(p)
        for a in range(2):
            low = recv[a, p, 2 * sc].reshape(ROWS, LANES).astype(F32)
            high = recv[a, p, 2 * sc + 1].reshape(ROWS, LANES).astype(F32)
            kv2[p, a, pl.ds(pl.multiple_of(seg * ROWS, ROWS), ROWS), :] = jnp.where(lane < DH, low, high).astype(BF16)
        start(lambda: grp_copy(
            seg_rows(p, seg), seg_rows(p, seg), z_s.at[p, 2], z_r.at[p, 2], at(xx, beside, core)))
        start(lambda: grp_copy(
            seg_rows(p, seg), seg_rows(p, seg), z_s.at[p, 3], z_r.at[p, zl % 2], at(xx, across, core)))
        start(lambda: grp_copy(seg_rows(p, seg), seg_rows(p, seg), f_s.at[p, 0], f_r.at[p, 0], mate_id))

    beside = zl + 1 - 2 * (zl % 2)
    across = 2 - zl // 2
    inner = ((zl + 1) // 2) % 2
    far = 2 * (1 - zl // 2)

    def relay(p, b):
        return grp_copy(
            seg_rows(p, (far + b) * 2 + core), seg_rows(p, (far + b) * 2 + core),
            y_s.at[p, b], y_r.at[p, b], at(xx, beside, core))

    def gather_pass(p):
        slot = seg_rows(p, beside * 2 + core)
        grp_copy(slot, slot, z_s.at[p, 2], z_r.at[p, 2], mate_id).wait_recv()
        start(lambda: grp_copy(
            seg_rows(p, beside * 2 + core), seg_rows(p, beside * 2 + core), f_s.at[p, 1], f_r.at[p, 1], mate_id))

        @pl.when(inner == 1)
        def _():
            for b in range(2):
                far_slot = seg_rows(p, (far + b) * 2 + core)
                grp_copy(far_slot, far_slot, z_s.at[p, 3], z_r.at[p, b], mate_id).wait_recv()
                relay(p, b).start()

        @pl.when(inner == 0)
        def _():
            for b in range(2):
                relay(p, b).wait_recv()

        for b in range(2):
            start(lambda b=b: grp_copy(
                seg_rows(p, (far + b) * 2 + core), seg_rows(p, (far + b) * 2 + core),
                f_s.at[p, 2 + b], f_r.at[p, 2 + b], mate_id))

    def gather_third(p):
        for j, z in enumerate((zl, beside, far, far + 1)):
            slot = seg_rows(p, z * 2 + mate)
            grp_copy(slot, slot, f_s.at[p, j], f_r.at[p, j], mate_id).wait_recv()
        sel = (iota((64, 1024), 1) == iota((64, 1024), 0) * 16 + pick3).astype(F32).astype(BF16)
        for a in range(2):
            kv2[p, a, pl.ds(pl.multiple_of(1024 + xx * 64, 64), 64), :] = nn(sel, kv2[p, a, 0:1024, :]).astype(BF16)
        for j in range(1, 4):
            start(lambda j=j: grp_copy(
                x_rows(p, xx), x_rows(p, xx), x_s.at[p, j], x_r.at[p, j], at(x_to(j), zl, core)))

    def gather_close(p):
        for j in range(1, 4):
            slot = x_rows(p, x_from(j))
            grp_copy(slot, slot, x_s.at[p, j], x_r.at[p, j], mate_id).wait_recv()

    taken3 = (iota((256, ROWS), 1) & 15) == pick3
    side = (iota((256, LANES), 1) < DH).astype(F32)
    sides = (side.astype(BF16), (1.0 - side).astype(BF16))

    def compute_chunk(p, ch, slot, special):
        qc = recv[2, p, pl.ds(ch * 2, 2)].reshape(256, LANES)
        gc = recv[3, p, pl.ds(ch * 2, 2)].reshape(256, LANES)
        g_t = nt(eye, gc)
        att_parts, dq_parts = [], []
        key_sum = value_sum = 0.0
        halves = [slice(h * 128, h * 128 + 128) for h in range(2)]
        heads = [slice(h * DH, h * DH + DH) for h in range(2)]
        qm = [qc * sides[h] for h in range(2)]
        gm = [gc * sides[h] for h in range(2)]
        tops, inverses, o_ts, deltas = [], [], [], []

        def merge(h, whole, part, combine):
            if h == 0:
                return jnp.concatenate([combine(whole[:, :128], part), whole[:, 128:]], axis=1)
            return jnp.concatenate([whole[:, :128], combine(whole[:, 128:], part)], axis=1)

        for h in range(2):
            score[h] = nt(recv[0, p].reshape(1024, LANES), qm[h])
            top = jnp.max(score[h], axis=0, keepdims=True)
            if special:
                wide = nt(kv2[p, 0], qm[h][halves[h]])
                score_b[h, 0:1024] = wide[0:1024]
                score_b[h, 1024:1280] = jnp.where(taken3, wide[1024:1280], LOWEST)
                top = merge(h, top, jnp.max(score_b[h], axis=0, keepdims=True), jnp.maximum)
            tops.append(top)
        for h in range(2):
            e = jnp.exp2((score[h] - tops[h]) * (SCALE * LOG2E))
            score[h] = e
            total = jnp.sum(e, axis=0, keepdims=True)
            if special:
                eb = jnp.exp2((score_b[h] - tops[h][:, halves[h]]) * (SCALE * LOG2E))
                score_b[h] = eb
                total = merge(h, total, jnp.sum(eb, axis=0, keepdims=True), jnp.add)
            inverses.append(1.0 / total)
        for h in range(2):
            prob[h] = (score[h] * inverses[h]).astype(BF16)
            if special:
                prob_b[h] = (score_b[h] * inverses[h][:, halves[h]]).astype(BF16)
        for h in range(2):
            o_t = nn(vt[heads[h]], prob[h])
            if special:
                o_t = merge(h, o_t, nn(vbt[heads[h]], prob_b[h]), jnp.add)
            a_t = o_t.astype(BF16).astype(F32)
            deltas.append(jnp.sum(a_t * g_t[heads[h]], axis=0, keepdims=True))
            att_parts.append(a_t)
            value_sum = value_sum + nn(prob[h], gm[h])
        for h in range(2):
            rise = nt(recv[1, p].reshape(1024, LANES), gm[h])
            slope[h] = ((score[h] * inverses[h]) * (rise - deltas[h])).astype(BF16)
            if special:
                rise_b = nt(kv2[p, 1], gm[h][halves[h]])
                slope_b[h] = ((score_b[h] * inverses[h][:, halves[h]]) * (rise_b - deltas[h][:, halves[h]])).astype(BF16)
        for h in range(2):
            dq_t = nn(kt[heads[h]], slope[h])
            if special:
                dq_t = merge(h, dq_t, nn(kbt[heads[h]], slope_b[h]), jnp.add)
            dq_parts.append(dq_t * SCALE)
            key_sum = key_sum + nn(slope[h], qm[h])
            if special:
                key_b = nn(slope_b[h], qm[h][halves[h]])
                value_b = nn(prob_b[h], gm[h][halves[h]])
                if h == 0:
                    acc2[p, 0], acc2[p, 1] = key_b, value_b
                else:
                    acc2[p, 0] += key_b
                    acc2[p, 1] += value_b
        acc[p, 0] += key_sum
        acc[p, 1] += value_sum
        out[0, p, pl.ds(slot * 2, 2)] = jnp.concatenate(att_parts, axis=0).T.astype(BF16).reshape(2, 8, 16, LANES)
        out[1, p, pl.ds(slot * 2, 2)] = jnp.concatenate(dq_parts, axis=0).T.astype(BF16).reshape(2, 8, 16, LANES)

    def compute(p, hooks):
        kt[...] = nt(eye, recv[0, p].reshape(1024, LANES)).astype(BF16)
        vt[...] = nt(eye, recv[1, p].reshape(1024, LANES)).astype(BF16)
        acc[p] = jnp.zeros_like(acc[p])
        sc = chunk_of(p)
        hooks[0]()

        @pl.loop(1, 4)
        def _(t):
            compute_chunk(p, (sc + t) % 4, t - 1, False)
            for when in range(1, 4):
                pl.when(t == when)(hooks[when])

    def compute_special(p):
        kbt[...] = nt(eye, kv2[p, 0]).astype(BF16)
        vbt[...] = nt(eye, kv2[p, 1]).astype(BF16)
        compute_chunk(p, chunk_of(p), 3, True)

    parts = ((0, 4), (4, 4)), ((0, 4), (4, 4)), ((0, 6), (6, 2)), ((0, 6), (6, 2))

    def p5_send(o, p, n):
        first, count = parts[o][n]
        part = slice(first, first + count)
        fin[o, s * 2 + p, part] = out[o, p, part, s]
        for j in TURNS:
            start(lambda j=j: seq_copy(
                out.at[o, p, part, s_to(j)], fin.at[o, s * 2 + p, part],
                p5_s.at[o, p, n, j], p5_r.at[o, p, n, j], s_to(j)))

    def p5_wait(o, p, n):
        first, count = parts[o][n]
        for j in TURNS:
            slot = fin.at[o, s_from(j) * 2 + p, first:first + count]
            seq_copy(slot, slot, p5_s.at[o, p, n, j], p5_r.at[o, p, n, j], s_to(j)).wait_recv()

    def p5_rest(a, p):
        sc = chunk_of(p)
        scale = SCALE if a == 0 else 1.0
        for u in range(3):
            rows = pl.ds(pl.multiple_of(((sc + u + 1) % 4) * 256, 256), 256)
            out[2 + a, p, 2 * u:2 * u + 2] = (acc[p, a, rows, :] * scale).astype(BF16).reshape(2, 8, 16, LANES)
        p5_send(2 + a, p, 0)

    def reduce_third(p):
        xs[p] = acc2[p, :, 1024:1280].astype(BF16)
        for j in range(1, 4):
            start(lambda j=j: grp_copy(
                xs.at[p, :, pl.ds(pl.multiple_of(x_to(j) * 64, 64), 64), :], xr.at[p, j],
                rx_s.at[p, j], rx_r.at[p, j], at(x_to(j), zl, core)))

    def reduce_core(p):
        for j in range(1, 4):
            grp_copy(xr.at[p, j], xr.at[p, j], rx_s.at[p, j], rx_r.at[p, j], mate_id).wait_recv()
        rows16 = iota((64, 16, LANES), 1) == pick3
        for a in range(2):
            third = acc2[p, a, pl.ds(pl.multiple_of(1024 + xx * 64, 64), 64), :]
            for j in range(1, 4):
                third = third + xr[p, j, a].astype(F32)
            spread = jnp.where(rows16, jnp.broadcast_to(third[:, None, :], (64, 16, LANES)), 0.0)
            acc2[p, a, 0:1024, :] += spread.reshape(1024, LANES)
        for a in range(2):
            for z in range(4):
                cs[p, a, z] = acc2[p, a, group_rows(z, mate), :].astype(BF16)
        start(lambda: grp_copy(cs.at[p], cr.at[p], rc_s.at[p], rc_r.at[p], mate_id))

    def group_rows(z, c):
        return pl.ds(pl.multiple_of((z * 2 + c) * ROWS, ROWS), ROWS)

    def reduce_seg(p):
        grp_copy(cr.at[p], cr.at[p], rc_s.at[p], rc_r.at[p], mate_id).wait_recv()
        for a in range(2):
            for z in range(4):
                zs[p, z, a] = (acc2[p, a, group_rows(z, core), :] + cr[p, a, z].astype(F32)).astype(BF16)
            own[p, a] = acc2[p, a, group_rows(zl, core), :] + cr[p, a, zl].astype(F32)
        for j in range(1, 4):
            start(lambda j=j: grp_copy(
                zs.at[p, z_to(j)], zr.at[p, j], rz_s.at[p, j], rz_r.at[p, j], at(xx, z_to(j), core)))

    def reduce_close(p):
        for j in range(1, 4):
            grp_copy(zr.at[p, j], zr.at[p, j], rz_s.at[p, j], rz_r.at[p, j], mate_id).wait_recv()
        special = pl.ds(pl.multiple_of(chunk_of(p) * 256, 256), 256)
        for a in range(2):
            total = own[p, a] + zr[p, 1, a].astype(F32) + zr[p, 2, a].astype(F32) + zr[p, 3, a].astype(F32)
            scale = SCALE if a == 0 else 1.0
            both = jnp.concatenate([jnp.where(lane < DH, total, 0.0), jnp.where(lane < DH, 0.0, total)], axis=0)
            out[2 + a, p, 6:8] = ((acc[p, a, special, :] + both) * scale).astype(BF16).reshape(2, 8, 16, LANES)
            p5_send(2 + a, p, 1)

    def restore(o, p):
        for b in range(8):
            at_lane = (b * 2 + p) * LANES
            turned = unperm[(b % 2) * 2 + p]
            result[o, :, at_lane:at_lane + LANES] = nn(turned, fin[o, b * 2 + p].reshape(ROWS, LANES)).astype(BF16)

    def first_half(p):
        p5_send(0, p, 0)
        p5_send(1, p, 0)

    def second_half(p):
        p5_send(0, p, 1)
        p5_send(1, p, 1)
        p5_rest(0, p)
        p5_rest(1, p)

    def nothing():
        pass

    def gather_rest(p):
        gather_pass(p)
        gather_third(p)
        gather_close(p)

    def first_2():
        gather_pass(0)
        gather_third(0)
        first_half(0)

    def first_3():
        gather_close(0)
        gather_pass(1)
        gather_third(1)

    def second_0():
        compute_special(1)
        reduce_third(1)

    def second_2():
        first_half(1)
        reduce_seg(1)

    p1_send(0, 1)
    p1_send(1, 1)
    gather_open(0)
    p1_send(2, 0)
    p1_send(3, 0)
    gather_open(1)
    p1_send(2, 1)
    p1_send(3, 1)
    p1_wait(2, 0)
    p1_wait(3, 0)
    compute(0, (nothing, nothing, first_2, first_3))
    compute_special(0)
    reduce_third(0)
    gather_close(1)
    reduce_core(0)
    reduce_seg(0)
    second_half(0)
    p1_wait(2, 1)
    p1_wait(3, 1)
    compute(1, (second_0, lambda: reduce_core(1), second_2, nothing))
    second_half(1)
    reduce_close(0)
    reduce_close(1)
    for o in range(4):
        for p in range(2):
            for n in range(2):
                p5_wait(o, p, n)
            restore(o, p)
        out_copy(o).start()
    for build in starts:
        build().wait_send()

    @pl.when(inner == 1)
    def _():
        for p in range(2):
            for b in range(2):
                relay(p, b).wait_send()

    for o in range(4):
        out_copy(o).wait()


def on_device(queries, keys, values, cotangent):
    shape = jax.ShapeDtypeStruct(queries.shape, queries.dtype)
    vm = pltpu.VMEM
    dma = pltpu.SemaphoreType.DMA
    scratch = [
        vm((4,) + queries.shape, BF16),
        vm((4,) + queries.shape, BF16),
        vm((4, 16, 8, 16, LANES), BF16),
        vm((4, 2, 8, 8, 16, LANES), BF16),
        vm((2, 2, 1280, LANES), BF16),
        vm((4, 2, 8, 8, 16, LANES), BF16),
        vm((4, 16, 8, 16, LANES), BF16),
        vm((2, 2, 256, LANES), BF16),
        vm((2, 4, 2, 64, LANES), BF16),
        vm((2, 2, 4, ROWS, LANES), BF16),
        vm((2, 2, 4, ROWS, LANES), BF16),
        vm((2, 4, 2, ROWS, LANES), BF16),
        vm((2, 4, 2, ROWS, LANES), BF16),
        vm((2, 1024, 256), F32),
        vm((2, 1280, ROWS), F32),
        vm((2, 1024, 256), BF16),
        vm((2, 1280, ROWS), BF16),
        vm((2, 1024, 256), BF16),
        vm((2, 1280, ROWS), BF16),
        vm((ROWS, 1024), BF16),
        vm((ROWS, 1024), BF16),
        vm((ROWS, 1280), BF16),
        vm((ROWS, 1280), BF16),
        vm((2, 2, 1024, LANES), F32),
        vm((2, 2, 1280, LANES), F32),
        vm((2, 2, ROWS, LANES), F32),
        dma((4, 2, 8)), dma((4, 2, 8)), dma((4, 2, 2, 8)), dma((4, 2, 2, 8)),
        dma((2, 4)), dma((2, 4)), dma((2, 4)), dma((2, 4)), dma((2, 4)), dma((2, 4)),
        dma((2, 4)), dma((2, 4)), dma((2,)), dma((2,)), dma((2, 4)), dma((2, 4)),
        dma((4,)), dma((4,)), dma((2, 2)), dma((2, 2)),
    ]
    return pl.pallas_call(
        kernel,
        out_shape=(shape,) * 4,
        in_specs=[pl.BlockSpec(memory_space=pl.ANY)] * 4,
        out_specs=(pl.BlockSpec(memory_space=pl.ANY),) * 4,
        scratch_shapes=scratch,
        compiler_params=pltpu.CompilerParams(
            collective_id=0, has_side_effects=True, vmem_limit_bytes=52 << 20),
    )(queries, keys, values, cotangent)


def solution(mesh):
    spec = P(("grp", "seq"), None)
    return jax.shard_map(
        on_device, mesh=mesh, in_specs=(spec,) * 4, out_specs=(spec,) * 4, check_vma=False)
```

```python
import functools

import jax
import jax.numpy as jnp
from jax import lax
from jax.experimental import pallas as pl
from jax.experimental.pallas import tpu as pltpu
from jax.sharding import PartitionSpec as P

DH = 64
MESH = pl.DeviceIdType.MESH
F32 = jnp.float32
BF16 = jnp.bfloat16
LOG2E = 1.4426950408889634
SCALE = 0.125
LOWEST = -1e30
CODES = 8
ROWS = 128
LANES = 128
TURNS = (1, 3, 5, 7, 2, 4, 6)


def nn(a, b):
    return jnp.dot(a, b, preferred_element_type=F32)


def nt(a, b):
    return lax.dot_general(a, b, (((1,), (1,)), ((), ())), preferred_element_type=F32)


def iota(shape, axis):
    return lax.broadcasted_iota(jnp.int32, shape, axis)


def kernel(
    q_hbm, k_hbm, v_hbm, g_hbm,
    att_hbm, dq_hbm, dk_hbm, dv_hbm,
    given, result,
    stage, recv, kv2, out, fin,
    xs, xr, cs, cr, zs, zr,
    score, score_b, prob, prob_b, slope, slope_b,
    kt, vt, kbt, vbt, acc, acc2, own,
    p1_s, p1_r, p5_s, p5_r, z_s, z_r, f_s, f_r, x_s, x_r,
    rx_s, rx_r, rc_s, rc_r, rz_s, rz_r,
    in_s, out_s, y_s, y_r,
):
    s = lax.axis_index("seq")
    grp = lax.axis_index("grp")
    core = grp % 2
    zl = (grp // 2) % 4
    xx = grp // 8
    seg = grp % 8
    mate = 1 - core
    pick3 = s // 2

    def at(x, z, c):
        return x * 8 + z * 2 + c

    def seq_copy(src, dst, ss, rs, to):
        return pltpu.make_async_remote_copy(
            src_ref=src, dst_ref=dst, send_sem=ss, recv_sem=rs,
            device_id={"seq": to}, device_id_type=MESH)

    def grp_copy(src, dst, ss, rs, to):
        return pltpu.make_async_remote_copy(
            src_ref=src, dst_ref=dst, send_sem=ss, recv_sem=rs,
            device_id={"grp": to}, device_id_type=MESH)

    mate_id = at(xx, zl, mate)

    def z_to(j):
        return (zl + j) % 4

    def z_from(j):
        return (zl + 4 - j) % 4

    def x_to(j):
        return (xx + j) % 4

    def x_from(j):
        return (xx + 4 - j) % 4

    def s_to(j):
        return (s + j) % 8

    def s_from(j):
        return (s + 8 - j) % 8

    def in_copy(a):
        return pltpu.make_async_copy((k_hbm, v_hbm, q_hbm, g_hbm)[a], given.at[a], in_s.at[a])

    def out_copy(o):
        return pltpu.make_async_copy(result.at[o], (att_hbm, dq_hbm, dk_hbm, dv_hbm)[o], out_s.at[o])

    for a in range(4):
        in_copy(a).start()

    barrier = pltpu.get_barrier_semaphore()
    for j in range(1, 8):
        pl.semaphore_signal(barrier, inc=1, device_id={"seq": s_to(j)}, device_id_type=MESH)
    for j in range(1, 4):
        pl.semaphore_signal(barrier, inc=1, device_id={"grp": at(xx, z_to(j), core)}, device_id_type=MESH)
        pl.semaphore_signal(barrier, inc=1, device_id={"grp": at(x_to(j), zl, core)}, device_id_type=MESH)
    pl.semaphore_signal(barrier, inc=1, device_id={"grp": mate_id}, device_id_type=MESH)

    ri, ci = iota((ROWS, ROWS), 0), iota((ROWS, ROWS), 1)
    perm = (ci == (ri & 15) * 8 + (ri >> 4)).astype(F32).astype(BF16)
    unperm = [
        (ci == (((ri & 7) - 2 * (turn + 1)) & 7) * 16 + (ri >> 3)).astype(F32).astype(BF16) for turn in range(4)]
    eye = (ri == ci).astype(F32).astype(BF16)

    starts = []

    def start(build):
        build().start()
        starts.append(build)

    def p1_send(a, p):
        for j in TURNS:
            start(lambda a=a, p=p, j=j: seq_copy(
                stage.at[a, s_to(j) * 2 + p], recv.at[a, p, :, s],
                p1_s.at[a, p, j], p1_r.at[a, p, j], s_to(j)))

    def p1_wait(a, p):
        for j in TURNS:
            slot = recv.at[a, p, :, s_from(j)]
            seq_copy(slot, slot, p1_s.at[a, p, j], p1_r.at[a, p, j], s_to(j)).wait_recv()

    for a in range(4):
        in_copy(a).wait()
        moved = nn(perm, given[a]).astype(BF16)
        for b in range(16):
            stage[a, b] = moved[:, b * LANES:(b + 1) * LANES].reshape(CODES, 16, LANES)
        for p in range(2):
            recv[a, p, :, s] = stage[a, s * 2 + p]
        if a == 0:
            pl.semaphore_wait(barrier, 14)
        if a < 2:
            p1_send(a, 0)

    def seg_rows(p, g):
        return kv2.at[p, :, pl.ds(pl.multiple_of(g * ROWS, ROWS), ROWS), :]

    def x_rows(p, x):
        return kv2.at[p, :, pl.ds(pl.multiple_of(1024 + x * 64, 64), 64), :]

    def chunk_of(p):
        return (s % 2) * 2 + p

    lane = iota((ROWS, LANES), 1)

    def gather_open(p):
        p1_wait(0, p)
        p1_wait(1, p)
        sc = chunk_of(p)
        for a in range(2):
            low = recv[a, p, 2 * sc].reshape(ROWS, LANES).astype(F32)
            high = recv[a, p, 2 * sc + 1].reshape(ROWS, LANES).astype(F32)
            kv2[p, a, pl.ds(pl.multiple_of(seg * ROWS, ROWS), ROWS), :] = jnp.where(lane < DH, low, high).astype(BF16)
        start(lambda: grp_copy(
            seg_rows(p, seg), seg_rows(p, seg), z_s.at[p, 2], z_r.at[p, 2], at(xx, beside, core)))
        start(lambda: grp_copy(
            seg_rows(p, seg), seg_rows(p, seg), z_s.at[p, 3], z_r.at[p, zl % 2], at(xx, across, core)))
        start(lambda: grp_copy(seg_rows(p, seg), seg_rows(p, seg), f_s.at[p, 0], f_r.at[p, 0], mate_id))

    beside = zl + 1 - 2 * (zl % 2)
    across = 2 - zl // 2
    inner = ((zl + 1) // 2) % 2
    far = 2 * (1 - zl // 2)

    def relay(p, b):
        return grp_copy(
            seg_rows(p, (far + b) * 2 + core), seg_rows(p, (far + b) * 2 + core),
            y_s.at[p, b], y_r.at[p, b], at(xx, beside, core))

    def gather_pass(p):
        slot = seg_rows(p, beside * 2 + core)
        grp_copy(slot, slot, z_s.at[p, 2], z_r.at[p, 2], mate_id).wait_recv()
        start(lambda: grp_copy(
            seg_rows(p, beside * 2 + core), seg_rows(p, beside * 2 + core), f_s.at[p, 1], f_r.at[p, 1], mate_id))

        @pl.when(inner == 1)
        def _():
            for b in range(2):
                far_slot = seg_rows(p, (far + b) * 2 + core)
                grp_copy(far_slot, far_slot, z_s.at[p, 3], z_r.at[p, b], mate_id).wait_recv()
                relay(p, b).start()

        @pl.when(inner == 0)
        def _():
            for b in range(2):
                relay(p, b).wait_recv()

        for b in range(2):
            start(lambda b=b: grp_copy(
                seg_rows(p, (far + b) * 2 + core), seg_rows(p, (far + b) * 2 + core),
                f_s.at[p, 2 + b], f_r.at[p, 2 + b], mate_id))

    def gather_third(p):
        for j, z in enumerate((zl, beside, far, far + 1)):
            slot = seg_rows(p, z * 2 + mate)
            grp_copy(slot, slot, f_s.at[p, j], f_r.at[p, j], mate_id).wait_recv()
        sel = (iota((64, 1024), 1) == iota((64, 1024), 0) * 16 + pick3).astype(F32).astype(BF16)
        for a in range(2):
            kv2[p, a, pl.ds(pl.multiple_of(1024 + xx * 64, 64), 64), :] = nn(sel, kv2[p, a, 0:1024, :]).astype(BF16)
        for j in range(1, 4):
            start(lambda j=j: grp_copy(
                x_rows(p, xx), x_rows(p, xx), x_s.at[p, j], x_r.at[p, j], at(x_to(j), zl, core)))

    def gather_close(p):
        for j in range(1, 4):
            slot = x_rows(p, x_from(j))
            grp_copy(slot, slot, x_s.at[p, j], x_r.at[p, j], mate_id).wait_recv()

    taken3 = (iota((256, ROWS), 1) & 15) == pick3
    side = (iota((256, LANES), 1) < DH).astype(F32)
    sides = (side.astype(BF16), (1.0 - side).astype(BF16))

    def compute_chunk(p, ch, slot, special):
        qc = recv[2, p, pl.ds(ch * 2, 2)].reshape(256, LANES)
        gc = recv[3, p, pl.ds(ch * 2, 2)].reshape(256, LANES)
        g_t = nt(eye, gc)
        att_parts, dq_parts = [], []
        key_sum = value_sum = 0.0
        halves = [slice(h * 128, h * 128 + 128) for h in range(2)]
        heads = [slice(h * DH, h * DH + DH) for h in range(2)]
        qm = [qc * sides[h] for h in range(2)]
        gm = [gc * sides[h] for h in range(2)]
        tops, inverses, o_ts, deltas = [], [], [], []

        def merge(h, whole, part, combine):
            if h == 0:
                return jnp.concatenate([combine(whole[:, :128], part), whole[:, 128:]], axis=1)
            return jnp.concatenate([whole[:, :128], combine(whole[:, 128:], part)], axis=1)

        for h in range(2):
            score[h] = nt(recv[0, p].reshape(1024, LANES), qm[h])
            top = jnp.max(score[h], axis=0, keepdims=True)
            if special:
                wide = nt(kv2[p, 0], qm[h][halves[h]])
                score_b[h, 0:1024] = wide[0:1024]
                score_b[h, 1024:1280] = jnp.where(taken3, wide[1024:1280], LOWEST)
                top = merge(h, top, jnp.max(score_b[h], axis=0, keepdims=True), jnp.maximum)
            tops.append(top)
        for h in range(2):
            e = jnp.exp2((score[h] - tops[h]) * (SCALE * LOG2E))
            score[h] = e
            total = jnp.sum(e, axis=0, keepdims=True)
            if special:
                eb = jnp.exp2((score_b[h] - tops[h][:, halves[h]]) * (SCALE * LOG2E))
                score_b[h] = eb
                total = merge(h, total, jnp.sum(eb, axis=0, keepdims=True), jnp.add)
            inverses.append(1.0 / total)
        for h in range(2):
            prob[h] = (score[h] * inverses[h]).astype(BF16)
            if special:
                prob_b[h] = (score_b[h] * inverses[h][:, halves[h]]).astype(BF16)
        for h in range(2):
            o_t = nn(vt[heads[h]], prob[h])
            if special:
                o_t = merge(h, o_t, nn(vbt[heads[h]], prob_b[h]), jnp.add)
            a_t = o_t.astype(BF16).astype(F32)
            deltas.append(jnp.sum(a_t * g_t[heads[h]], axis=0, keepdims=True))
            att_parts.append(a_t)
            value_sum = value_sum + nn(prob[h], gm[h])
        for h in range(2):
            rise = nt(recv[1, p].reshape(1024, LANES), gm[h])
            slope[h] = ((score[h] * inverses[h]) * (rise - deltas[h])).astype(BF16)
            if special:
                rise_b = nt(kv2[p, 1], gm[h][halves[h]])
                slope_b[h] = ((score_b[h] * inverses[h][:, halves[h]]) * (rise_b - deltas[h][:, halves[h]])).astype(BF16)
        for h in range(2):
            dq_t = nn(kt[heads[h]], slope[h])
            if special:
                dq_t = merge(h, dq_t, nn(kbt[heads[h]], slope_b[h]), jnp.add)
            dq_parts.append(dq_t * SCALE)
            key_sum = key_sum + nn(slope[h], qm[h])
            if special:
                key_b = nn(slope_b[h], qm[h][halves[h]])
                value_b = nn(prob_b[h], gm[h][halves[h]])
                if h == 0:
                    acc2[p, 0], acc2[p, 1] = key_b, value_b
                else:
                    acc2[p, 0] += key_b
                    acc2[p, 1] += value_b
        acc[p, 0] += key_sum
        acc[p, 1] += value_sum
        out[0, p, pl.ds(slot * 2, 2)] = jnp.concatenate(att_parts, axis=0).T.astype(BF16).reshape(2, 8, 16, LANES)
        out[1, p, pl.ds(slot * 2, 2)] = jnp.concatenate(dq_parts, axis=0).T.astype(BF16).reshape(2, 8, 16, LANES)

    def compute(p, hooks):
        kt[...] = nt(eye, recv[0, p].reshape(1024, LANES)).astype(BF16)
        vt[...] = nt(eye, recv[1, p].reshape(1024, LANES)).astype(BF16)
        acc[p] = jnp.zeros_like(acc[p])
        sc = chunk_of(p)
        hooks[0]()

        @pl.loop(1, 4)
        def _(t):
            compute_chunk(p, (sc + t) % 4, t - 1, False)
            for when in range(1, 4):
                pl.when(t == when)(hooks[when])

    def compute_special(p):
        kbt[...] = nt(eye, kv2[p, 0]).astype(BF16)
        vbt[...] = nt(eye, kv2[p, 1]).astype(BF16)
        compute_chunk(p, chunk_of(p), 3, True)

    parts = ((0, 4), (4, 4)), ((0, 4), (4, 4)), ((0, 6), (6, 2)), ((0, 6), (6, 2))

    def p5_send(o, p, n):
        first, count = parts[o][n]
        part = slice(first, first + count)
        fin[o, s * 2 + p, part] = out[o, p, part, s]
        for j in TURNS:
            start(lambda j=j: seq_copy(
                out.at[o, p, part, s_to(j)], fin.at[o, s * 2 + p, part],
                p5_s.at[o, p, n, j], p5_r.at[o, p, n, j], s_to(j)))

    def p5_wait(o, p, n):
        first, count = parts[o][n]
        for j in TURNS:
            slot = fin.at[o, s_from(j) * 2 + p, first:first + count]
            seq_copy(slot, slot, p5_s.at[o, p, n, j], p5_r.at[o, p, n, j], s_to(j)).wait_recv()

    def p5_rest(a, p):
        sc = chunk_of(p)
        scale = SCALE if a == 0 else 1.0
        for u in range(3):
            rows = pl.ds(pl.multiple_of(((sc + u + 1) % 4) * 256, 256), 256)
            out[2 + a, p, 2 * u:2 * u + 2] = (acc[p, a, rows, :] * scale).astype(BF16).reshape(2, 8, 16, LANES)
        p5_send(2 + a, p, 0)

    def reduce_third(p):
        xs[p] = acc2[p, :, 1024:1280].astype(BF16)
        for j in range(1, 4):
            start(lambda j=j: grp_copy(
                xs.at[p, :, pl.ds(pl.multiple_of(x_to(j) * 64, 64), 64), :], xr.at[p, j],
                rx_s.at[p, j], rx_r.at[p, j], at(x_to(j), zl, core)))

    def reduce_core(p):
        for j in range(1, 4):
            grp_copy(xr.at[p, j], xr.at[p, j], rx_s.at[p, j], rx_r.at[p, j], mate_id).wait_recv()
        rows16 = iota((64, 16, LANES), 1) == pick3
        for a in range(2):
            third = acc2[p, a, pl.ds(pl.multiple_of(1024 + xx * 64, 64), 64), :]
            for j in range(1, 4):
                third = third + xr[p, j, a].astype(F32)
            spread = jnp.where(rows16, jnp.broadcast_to(third[:, None, :], (64, 16, LANES)), 0.0)
            acc2[p, a, 0:1024, :] += spread.reshape(1024, LANES)
        for a in range(2):
            for z in range(4):
                cs[p, a, z] = acc2[p, a, group_rows(z, mate), :].astype(BF16)
        start(lambda: grp_copy(cs.at[p], cr.at[p], rc_s.at[p], rc_r.at[p], mate_id))

    def group_rows(z, c):
        return pl.ds(pl.multiple_of((z * 2 + c) * ROWS, ROWS), ROWS)

    def reduce_seg(p):
        grp_copy(cr.at[p], cr.at[p], rc_s.at[p], rc_r.at[p], mate_id).wait_recv()
        for a in range(2):
            for z in range(4):
                zs[p, z, a] = (acc2[p, a, group_rows(z, core), :] + cr[p, a, z].astype(F32)).astype(BF16)
            own[p, a] = acc2[p, a, group_rows(zl, core), :] + cr[p, a, zl].astype(F32)
        for j in range(1, 4):
            start(lambda j=j: grp_copy(
                zs.at[p, z_to(j)], zr.at[p, j], rz_s.at[p, j], rz_r.at[p, j], at(xx, z_to(j), core)))

    def reduce_close(p):
        for j in range(1, 4):
            grp_copy(zr.at[p, j], zr.at[p, j], rz_s.at[p, j], rz_r.at[p, j], mate_id).wait_recv()
        special = pl.ds(pl.multiple_of(chunk_of(p) * 256, 256), 256)
        for a in range(2):
            total = own[p, a] + zr[p, 1, a].astype(F32) + zr[p, 2, a].astype(F32) + zr[p, 3, a].astype(F32)
            scale = SCALE if a == 0 else 1.0
            both = jnp.concatenate([jnp.where(lane < DH, total, 0.0), jnp.where(lane < DH, 0.0, total)], axis=0)
            out[2 + a, p, 6:8] = ((acc[p, a, special, :] + both) * scale).astype(BF16).reshape(2, 8, 16, LANES)
            p5_send(2 + a, p, 1)

    def restore(o, p):
        for b in range(8):
            at_lane = (b * 2 + p) * LANES
            turned = unperm[(b % 2) * 2 + p]
            result[o, :, at_lane:at_lane + LANES] = nn(turned, fin[o, b * 2 + p].reshape(ROWS, LANES)).astype(BF16)

    def first_half(p):
        p5_send(0, p, 0)
        p5_send(1, p, 0)

    def second_half(p):
        p5_send(0, p, 1)
        p5_send(1, p, 1)
        p5_rest(0, p)
        p5_rest(1, p)

    def nothing():
        pass

    def gather_rest(p):
        gather_pass(p)
        gather_third(p)
        gather_close(p)

    def first_2():
        gather_pass(0)
        gather_third(0)
        first_half(0)

    def first_3():
        gather_close(0)
        gather_pass(1)
        gather_third(1)

    def second_0():
        compute_special(1)
        reduce_third(1)

    def second_2():
        reduce_seg(1)
        first_half(1)

    p1_send(0, 1)
    p1_send(1, 1)
    gather_open(0)
    p1_send(2, 0)
    p1_send(3, 0)
    gather_open(1)
    p1_send(2, 1)
    p1_send(3, 1)
    p1_wait(2, 0)
    p1_wait(3, 0)
    compute(0, (nothing, nothing, first_2, first_3))
    compute_special(0)
    reduce_third(0)
    gather_close(1)
    reduce_core(0)
    reduce_seg(0)
    second_half(0)
    p1_wait(2, 1)
    p1_wait(3, 1)
    compute(1, (second_0, lambda: reduce_core(1), second_2, nothing))
    second_half(1)
    reduce_close(0)
    reduce_close(1)
    for p in range(2):
        for o in range(4):
            for n in range(2):
                p5_wait(o, p, n)
            restore(o, p)
            if p == 1:
                out_copy(o).start()
    for build in starts:
        build().wait_send()

    @pl.when(inner == 1)
    def _():
        for p in range(2):
            for b in range(2):
                relay(p, b).wait_send()

    for o in range(4):
        out_copy(o).wait()


def on_device(queries, keys, values, cotangent):
    shape = jax.ShapeDtypeStruct(queries.shape, queries.dtype)
    vm = pltpu.VMEM
    dma = pltpu.SemaphoreType.DMA
    scratch = [
        vm((4,) + queries.shape, BF16),
        vm((4,) + queries.shape, BF16),
        vm((4, 16, 8, 16, LANES), BF16),
        vm((4, 2, 8, 8, 16, LANES), BF16),
        vm((2, 2, 1280, LANES), BF16),
        vm((4, 2, 8, 8, 16, LANES), BF16),
        vm((4, 16, 8, 16, LANES), BF16),
        vm((2, 2, 256, LANES), BF16),
        vm((2, 4, 2, 64, LANES), BF16),
        vm((2, 2, 4, ROWS, LANES), BF16),
        vm((2, 2, 4, ROWS, LANES), BF16),
        vm((2, 4, 2, ROWS, LANES), BF16),
        vm((2, 4, 2, ROWS, LANES), BF16),
        vm((2, 1024, 256), F32),
        vm((2, 1280, ROWS), F32),
        vm((2, 1024, 256), BF16),
        vm((2, 1280, ROWS), BF16),
        vm((2, 1024, 256), BF16),
        vm((2, 1280, ROWS), BF16),
        vm((ROWS, 1024), BF16),
        vm((ROWS, 1024), BF16),
        vm((ROWS, 1280), BF16),
        vm((ROWS, 1280), BF16),
        vm((2, 2, 1024, LANES), F32),
        vm((2, 2, 1280, LANES), F32),
        vm((2, 2, ROWS, LANES), F32),
        dma((4, 2, 8)), dma((4, 2, 8)), dma((4, 2, 2, 8)), dma((4, 2, 2, 8)),
        dma((2, 4)), dma((2, 4)), dma((2, 4)), dma((2, 4)), dma((2, 4)), dma((2, 4)),
        dma((2, 4)), dma((2, 4)), dma((2,)), dma((2,)), dma((2, 4)), dma((2, 4)),
        dma((4,)), dma((4,)), dma((2, 2)), dma((2, 2)),
    ]
    return pl.pallas_call(
        kernel,
        out_shape=(shape,) * 4,
        in_specs=[pl.BlockSpec(memory_space=pl.ANY)] * 4,
        out_specs=(pl.BlockSpec(memory_space=pl.ANY),) * 4,
        scratch_shapes=scratch,
        compiler_params=pltpu.CompilerParams(
            collective_id=0, has_side_effects=True, vmem_limit_bytes=52 << 20),
    )(queries, keys, values, cotangent)


def solution(mesh):
    spec = P(("grp", "seq"), None)
    return jax.shard_map(
        on_device, mesh=mesh, in_specs=(spec,) * 4, out_specs=(spec,) * 4, check_vma=False)
```
